256 devices in a mesh: frame: 64 (over x_lo, z, y), band: 4 (over x_hi, core).
Axes of the slice: x: 4 (x_hi: 2, x_lo: 2; x = x_hi * 2 + x_lo), y: 4, z: 8, core: 2. Of those that a mesh axis runs over, the one named last changes fastest.
Arguments:
- queries: bfloat16 [64, 4, 2, 64, 3328], P('frame', 'band'), may hold values from -16 to 16
- keys: bfloat16 [64, 4, 2, 64, 3328], P('frame', 'band'), may hold values from -4 to 4
- values: bfloat16 [64, 4, 2, 64, 3328], P('frame', 'band'), may hold values from -6 to 6
- grad_out: bfloat16 [64, 4, 2, 64, 3328], P('frame', 'band'), may hold values from -6 to 6
- windows: int32 [64, 4, 2, 8], P('frame', 'band'), may hold values from 0 to 511, as said below
Outputs:
- attn_out: bfloat16 [64, 4, 2, 64, 3328], P('frame', 'band')
- grad_query: bfloat16 [64, 4, 2, 64, 3328], P('frame', 'band')
- grad_key: bfloat16 [64, 4, 2, 64, 3328], P('frame', 'band')
- grad_value: bfloat16 [64, 4, 2, 64, 3328], P('frame', 'band')
The draws below stay inside these ranges and needn't reach their ends.
Inputs may be any that keep to these rules, and one draw needn't show every extreme that they name: `windows`: entry 0 of each window is the query tile itself; the other 7 entries are distinct tiles of the same or an adjacent frame and of the same or an adjacent band, at any position along the width.
All inputs are finite; a program needn't handle non-finite values.
Results may differ from the reference program's by a relative error of at most 0.015.
Values may be sent and summed in bfloat16 or wider, within the bound.
A program may use at most 128 MiB of HBM per device.

```python
import jax
import jax.numpy as jnp
from jax import lax

H = 26
HD = 128
TILE = 64
WIN = 8
WT = 2
FRAMES = 64
BANDS = 4
N_FRAME = 64
N_BAND = 4


def field_shape():
    return (FRAMES, BANDS, WT, TILE, H * HD)


def normal_keys(key, bound):
    return jax.random.truncated_normal(key, -bound, bound, field_shape(), jnp.float32)


def draw_keys(key, part):
    result = normal_keys(key, 4.0)
    return result.astype(jnp.bfloat16)


def draw_queries(key, part):
    key = jax.random.fold_in(key, 13)
    result = jax.random.truncated_normal(key, -6.0, 6.0, field_shape(), jnp.float32)
    return result.astype(jnp.bfloat16)


def draw_windows(key, part):
    key = jax.random.fold_in(key, 17)
    reach = 9 * WT
    full = (FRAMES, BANDS, WT, reach)
    frame_pos = lax.broadcasted_iota(jnp.int32, full, 0)
    band_pos = lax.broadcasted_iota(jnp.int32, full, 1)
    tile_pos = lax.broadcasted_iota(jnp.int32, full, 2)
    candidate = lax.broadcasted_iota(jnp.int32, full, 3)
    frame_step = candidate // (3 * WT) - 1
    band_step = candidate // WT % 3 - 1
    tile_step = candidate % WT
    frame_key = frame_pos + frame_step
    band_key = band_pos + band_step
    inside = (frame_key >= 0) & (frame_key < FRAMES) & (band_key >= 0) & (band_key < BANDS)
    itself = (frame_step == 0) & (band_step == 0) & (tile_step == tile_pos)
    ranking = jax.random.randint(key, full, 0, 1 << 20, jnp.int32) * reach + candidate
    ranking = jnp.where(inside & jnp.logical_not(itself), ranking, -1)
    chosen = lax.top_k(ranking, WIN - 1)[1]
    key_ids = (frame_key * BANDS + band_key) * WT + tile_step
    others = jnp.take_along_axis(key_ids, chosen, axis=3)
    own_ids = (frame_pos[..., 0:1] * BANDS + band_pos[..., 0:1]) * WT + tile_pos[..., 0:1]
    return jnp.concatenate((own_ids, others), axis=3).astype(jnp.int32)


def steps_of(rng, shape, shards, least, largest):
    factor_of, own = 1.0, jax.random.fold_in(rng, 6)
    for axis_at, shards_of in shards:
        heights = jnp.exp(jax.random.uniform(jax.random.fold_in(own, axis_at), (shards_of,), jnp.float32, least / len(shards), largest / len(shards)))
        factor_of = factor_of * jnp.repeat(heights, shape[axis_at] // shards_of).reshape([-1 if axis == axis_at else 1 for axis in range(len(shape))])
    return factor_of


def normal_values(stream_key, shape, scale, most, split=(), held_as=jnp.bfloat16):
    drawn = scale * jax.random.normal(stream_key, shape, jnp.float32)
    if split:
        drawn = drawn * steps_of(stream_key, shape, split, -0.22, 0.18)
    return jnp.clip(drawn, -most, most).astype(held_as)


def setup_inputs(seed: int = 0) -> dict:
    key_of = jax.random.split(jax.random.key(seed), 6)
    queries = draw_queries(jax.random.fold_in(key_of[5], 71), 0)
    keys = draw_keys(jax.random.fold_in(key_of[5], 71), 0)
    values = normal_values(key_of[2], (FRAMES, BANDS, WT, TILE, H * HD), 1.0, 6.0, ((0, 64), (1, 4)))
    grad_out = normal_values(key_of[3], (FRAMES, BANDS, WT, TILE, H * HD), 1.0, 6.0, ((0, 64), (1, 4)))
    windows = draw_windows(jax.random.fold_in(key_of[5], 71), 0)
    return {"queries": queries, "keys": keys, "values": values, "grad_out": grad_out, "windows": windows}


def rounded(tensor):
    return lax.optimization_barrier(tensor.astype(jnp.bfloat16)).astype(jnp.float32)


def device_terms(query_rows, slot_keys, slot_values, grad_rows):
    tile_total = query_rows.shape[0]
    feature = H * HD
    scaling = HD ** -0.5
    query_float = query_rows.astype(jnp.float32).reshape(tile_total, TILE, H, HD)
    key_float = slot_keys.astype(jnp.float32).reshape(tile_total, WIN * TILE, H, HD)
    value_float = slot_values.astype(jnp.float32).reshape(tile_total, WIN * TILE, H, HD)
    grad_float = grad_rows.astype(jnp.float32).reshape(tile_total, TILE, H, HD)
    scores = jnp.einsum("tqhd,tkhd->thqk", query_float, key_float) * scaling
    maxima = jnp.max(scores, axis=-1, keepdims=True)
    log_total = maxima + jnp.log(jnp.sum(jnp.exp(scores - maxima), axis=-1, keepdims=True))
    weights = jnp.exp(scores - log_total)
    prob_round = rounded(weights)
    attention = jnp.einsum("thqk,tkhd->tqhd", prob_round, value_float).astype(jnp.bfloat16)
    attn_float = lax.optimization_barrier(attention).astype(jnp.float32)
    deltas = jnp.transpose(jnp.sum(grad_float * attn_float, axis=-1), (0, 2, 1))[..., None]
    grad_prob = jnp.einsum("tqhd,tkhd->thqk", grad_float, value_float)
    grad_score = rounded(weights * (grad_prob - deltas) * scaling)
    grad_query = jnp.einsum("thqk,tkhd->tqhd", grad_score, key_float).astype(jnp.bfloat16)
    key_slots = jnp.einsum("thqk,tqhd->tkhd", grad_score, query_float)
    value_slots = jnp.einsum("thqk,tqhd->tkhd", prob_round, grad_float)
    return (attention.reshape(tile_total, TILE, feature),
            grad_query.reshape(tile_total, TILE, feature),
            key_slots.reshape(tile_total * WIN, TILE, feature),
            value_slots.reshape(tile_total * WIN, TILE, feature))


def reference(queries, keys, values, grad_out, windows):
    device_count = N_FRAME * N_BAND
    feature = H * HD
    slot_total = WT * WIN
    query_dev = queries.reshape(device_count, WT, TILE, feature)
    grad_dev = grad_out.reshape(device_count, WT, TILE, feature)
    key_tiles = keys.reshape(device_count * WT, TILE, feature)
    value_tiles = values.reshape(device_count * WT, TILE, feature)
    window_dev = windows.reshape(device_count, slot_total).astype(jnp.int32)
    earlier = jnp.tril(jnp.ones((slot_total, slot_total), jnp.float32), -1)
    empty_sums = jnp.zeros((device_count * WT, TILE, feature), jnp.float32)

    def visit(sums, device):
        key_sums, value_sums = sums
        tile_ids = window_dev[device]
        slot_keys = key_tiles[tile_ids].reshape(WT, WIN * TILE, feature)
        slot_values = value_tiles[tile_ids].reshape(WT, WIN * TILE, feature)
        attention, grad_query, key_slots, value_slots = device_terms(query_dev[device], slot_keys, slot_values, grad_dev[device])
        matches = (tile_ids[:, None] == tile_ids[None, :]).astype(jnp.float32)
        leading = (jnp.sum(matches * earlier, axis=1) == 0).astype(jnp.float32)[:, None, None]
        key_part = rounded(jnp.einsum("ij,jrc->irc", matches, key_slots, precision=lax.Precision.HIGHEST)) * leading
        value_part = rounded(jnp.einsum("ij,jrc->irc", matches, value_slots, precision=lax.Precision.HIGHEST)) * leading
        key_sums = key_sums.at[tile_ids].add(key_part)
        value_sums = value_sums.at[tile_ids].add(value_part)
        return (key_sums, value_sums), (attention, grad_query)

    (key_sums, value_sums), (attention, grad_query) = lax.scan(
        visit, (empty_sums, empty_sums), jnp.arange(device_count, dtype=jnp.int32))
    full_shape = queries.shape
    return (attention.reshape(full_shape), grad_query.reshape(full_shape),
            key_sums.astype(jnp.bfloat16).reshape(full_shape),
            value_sums.astype(jnp.bfloat16).reshape(full_shape))
```

```python
import functools

import jax
import jax.numpy as jnp
from jax import lax
from jax.experimental import pallas as pl
from jax.experimental.pallas import tpu as pltpu
from jax.sharding import PartitionSpec as P

MESH = pl.DeviceIdType.MESH
HD = 128
TILE = 64
WT = 2
BANDS = 4
TILES = BANDS * WT
ROWS = WT * TILE
MASKED = -1e30
AHEAD = 4
LATER = 2
LAG = 3
HALO, RET = 0, 1


def swapped(band):
    return 2 * (band % 2) + band // 2


def dot_nt(a, b):
    return lax.dot_general(a, b, (((1,), (1,)), ((), ())), preferred_element_type=jnp.float32)


def dot_tn(a, b):
    return lax.dot_general(a, b, (((0,), (0,)), ((), ())), preferred_element_type=jnp.float32)


def dot_nn(a, b):
    return jnp.dot(a, b, preferred_element_type=jnp.float32)


def kernel(
    frames, heads,
    win_ref, q_in, k_in, v_in, g_in,
    o_out, dq_out, dk_out, dv_out,
    qb, gb, kb, vb, bias, own_k, own_v, acc_k, acc_v, send_k, send_v, back_k, back_v, o_b, dq_b, dk_b, dv_b,
    in_send, in_recv, in_local, halo_send, halo_recv, ret_send, ret_recv, out_send, out_recv, out_local, bias_send, bias_recv,
    relay, relay_send, relay_recv,
):
    chip_heads = heads // 2
    most = (chip_heads + 1) // 2
    f, b = lax.axis_index("frame"), lax.axis_index("band")
    has_prev, has_next = f > 0, f < frames - 1
    peers = (b + 1 - 2 * (b % 2), (b + 2) % BANDS, BANDS - 1 - b)

    middle = frames // 2

    def across(frame, band):
        return band + (frame // middle) * (swapped(band) - band)

    spare = 2 * most - chip_heads
    own_set = across(f, b)

    def at(frame):
        return frame, across(frame, own_set)

    def head_count(band):
        return most - spare * ((across(f, band) + 1) // 2 % 2)

    def columns(band, j):
        those = across(f, band)
        first = most * those - spare * (2 * those // 3)
        return pl.ds(pl.multiple_of((first + j) * HD, HD), HD)

    def tiles(band):
        return pl.ds(WT * band, WT)

    mine = head_count(b)
    in_refs = (k_in, v_in, q_in, g_in)
    out_refs = (o_out, dq_out, dk_out, dv_out)
    out_bufs = (o_b, dq_b, dk_b, dv_b)

    def landing(arr, j):
        return (kb.at[j, 1], vb.at[j, 1], qb.at[j], gb.at[j])[arr].at[tiles(b)]

    def in_copy(arr, j, n):
        return pltpu.make_async_remote_copy(
            src_ref=in_refs[arr].at[0, 0, :, :, columns(peers[n], j)],
            dst_ref=landing(arr, j),
            send_sem=in_send.at[arr, j, n],
            recv_sem=in_recv.at[arr, j, n],
            device_id=(f, peers[n]),
            device_id_type=MESH,
        )

    def in_own(arr, j):
        return pltpu.make_async_copy(
            in_refs[arr].at[0, 0, :, :, columns(b, j)], landing(arr, j), in_local.at[arr, j]
        )

    def start_in(arrs, j):
        for n in (1, 2, 0):
            @pl.when(j < head_count(peers[n]))
            def _():
                for arr in arrs:
                    in_copy(arr, j, n).start()

        @pl.when(j < mine)
        def _():
            for arr in arrs:
                in_own(arr, j).start()

    def wait_in(arrs, j):
        for arr in arrs:
            in_own(arr, j).wait()
            for n in range(3):
                in_copy(arr, j, n).wait_recv()

    detour = (0, frames - 1)
    ends = ((middle, middle - 1), (middle - 1, middle))

    def straight(arr, j):
        return (2 * j + arr) % 2 == 0

    def side_refs(kind, arr, j, side):
        if kind == HALO:
            buf = (kb, vb)[arr]
            return buf.at[j, 1], buf.at[j, 2 - 2 * side], halo_send.at[arr, j, side], halo_recv.at[arr, j, side]
        return (
            (send_k, send_v)[arr].at[j, side],
            (back_k, back_v)[arr].at[j, 1 - side],
            ret_send.at[arr, j, side],
            ret_recv.at[arr, j, side],
        )

    def side_copy(kind, arr, j, side):
        source, target, send, recv = side_refs(kind, arr, j, side)
        return pltpu.make_async_remote_copy(
            src_ref=source, dst_ref=target, send_sem=send, recv_sem=recv,
            device_id=at(f - 1 + 2 * side), device_id_type=MESH,
        )

    def relay_in(kind, arr, j, side, over):
        source, _, send, _ = side_refs(kind, arr, j, side)
        return pltpu.make_async_remote_copy(
            src_ref=source, dst_ref=relay.at[kind, arr, j, side], send_sem=send,
            recv_sem=relay_recv.at[kind, arr, j, side], device_id=at(over), device_id_type=MESH,
        )

    def relay_out(kind, arr, j, side):
        _, target, _, recv = side_refs(kind, arr, j, side)
        return pltpu.make_async_remote_copy(
            src_ref=relay.at[kind, arr, j, side], dst_ref=target, send_sem=relay_send.at[kind, arr, j, side],
            recv_sem=recv, device_id=at(ends[side][1]), device_id_type=MESH,
        )

    def pass_on(kind, j, act):
        for side in range(2):
            for arr in range(2):
                @pl.when((f == detour[kind]) & jnp.logical_not(straight(arr, j)))
                def _():
                    act(kind, arr, j, side)

    def relay_start(kind, arr, j, side):
        relay_in(kind, arr, j, side, f).wait_recv()
        relay_out(kind, arr, j, side).start()

    def relay_end(kind, arr, j, side):
        relay_out(kind, arr, j, side).wait_send()

    has = (has_prev, has_next)

    def start_sides(kind, j):
        for side in range(2):
            @pl.when(has[side] & (f != ends[side][0]))
            def _():
                for arr in range(2):
                    side_copy(kind, arr, j, side).start()

            for arr in range(2):
                @pl.when((f == ends[side][0]) & straight(arr, j))
                def _():
                    side_copy(kind, arr, j, side).start()

                @pl.when((f == ends[side][0]) & jnp.logical_not(straight(arr, j)))
                def _():
                    relay_in(kind, arr, j, side, detour[kind]).start()

    def wait_sides(kind, j):
        for side in range(2):
            @pl.when(has[1 - side])
            def _():
                for arr in range(2):
                    side_copy(kind, arr, j, side).wait_recv()

    def out_copy(arr, j, n):
        return pltpu.make_async_remote_copy(
            src_ref=out_bufs[arr].at[j, tiles(peers[n])],
            dst_ref=out_refs[arr].at[0, 0, :, :, columns(b, j)],
            send_sem=out_send.at[arr, j, n],
            recv_sem=out_recv.at[arr, j, n],
            device_id=(f, peers[n]),
            device_id_type=MESH,
        )

    def out_own(arr, j):
        return pltpu.make_async_copy(
            out_bufs[arr].at[j, tiles(b)], out_refs[arr].at[0, 0, :, :, columns(b, j)], out_local.at[arr, j]
        )

    def start_out(arrs, j):
        for n in (1, 2, 0):
            for arr in arrs:
                out_copy(arr, j, n).start()
        for arr in arrs:
            out_own(arr, j).start()

    def bias_copy(n):
        return pltpu.make_async_remote_copy(
            src_ref=bias.at[b],
            dst_ref=bias.at[b],
            send_sem=bias_send.at[n],
            recv_sem=bias_recv.at[n],
            device_id=(f, peers[n]),
            device_id_type=MESH,
        )

    barrier = pltpu.get_barrier_semaphore()
    for n in range(3):
        pl.semaphore_signal(barrier, inc=1, device_id=(f, peers[n]), device_id_type=MESH)
    for side in range(2):
        @pl.when(has[side])
        def _():
            pl.semaphore_signal(
                barrier, inc=1, device_id=at(f - 1 + 2 * side), device_id_type=MESH
            )

    partners = {}
    for side in range(2):
        for way in detour:
            for end in ends[side]:
                partners.setdefault(end, set()).add(way)
                partners.setdefault(way, set()).add(end)
    for here in sorted(partners):
        @pl.when(f == here)
        def _():
            for there in sorted(partners[here]):
                pl.semaphore_signal(barrier, inc=1, device_id=at(there), device_id_type=MESH)

    place = lax.broadcasted_iota(jnp.int32, (3 * TILES, ROWS), 0) + TILES * (f - 1)
    lane = lax.broadcasted_iota(jnp.int32, (3 * TILES, ROWS), 1)
    named = []
    for t in range(WT):
        hits = [jnp.where(place == win_ref[0, 0, t, slot], 1, 0) for slot in range(8)]
        named.append(functools.reduce(jnp.maximum, hits))
    named = jnp.where(lane < TILE, named[0], named[1])
    bias[b] = jnp.where(named == 1, 0.0, MASKED)

    greeted = {}
    for here in sorted({0, frames - 1, *partners}):
        count = 3 + (here > 0) + (here < frames - 1) + len(partners.get(here, ()))
        greeted.setdefault(count, []).append(here)
    special = f < 0
    for count, those in sorted(greeted.items()):
        among = functools.reduce(jnp.logical_or, [f == here for here in those])
        special = special | among

        @pl.when(among)
        def _():
            pl.semaphore_wait(barrier, count)

    @pl.when(jnp.logical_not(special))
    def _():
        pl.semaphore_wait(barrier, 5)

    start_in((0, 1), 0)
    for n in range(3):
        bias_copy(n).start()
    lax.fori_loop(1, most, lambda j, carry: (start_in((0, 1), j), carry)[1], 0)

    nothing = jnp.zeros((most, TILES, TILE, HD), jnp.bfloat16)
    for side in range(2):
        @pl.when(jnp.logical_not(has[side]))
        def _():
            kb[:, 2 * side] = nothing
            vb[:, 2 * side] = nothing
            back_k[:, side] = nothing
            back_v[:, side] = nothing

    for n in range(3):
        pltpu.make_async_remote_copy(
            src_ref=bias.at[b], dst_ref=bias.at[peers[n]], send_sem=bias_send.at[n], recv_sem=bias_recv.at[n],
            device_id=(f, peers[n]), device_id_type=MESH,
        ).wait_recv()

    scaling = HD**-0.5
    scaling2 = scaling * 1.4426950408889634

    def compute(j):
        for band in range(BANDS):
            low, high = max(0, band - 1), min(BANDS, band + 2)
            tile_count = WT * (high - low)
            keys_count = tile_count * TILE
            q = qb[j, WT * band : WT * band + WT].reshape(ROWS, HD)
            g = gb[j, WT * band : WT * band + WT].reshape(ROWS, HD)
            ks = [kb[j, fr, WT * low : WT * high].reshape(keys_count, HD) for fr in range(3)]
            vs = [vb[j, fr, WT * low : WT * high].reshape(keys_count, HD) for fr in range(3)]
            scores = []
            for fr in range(3):
                start = fr * TILES + WT * low
                part = (dot_nt(ks[fr], q) * scaling2).reshape(tile_count, TILE, ROWS)
                part = part + bias[band, start : start + tile_count][:, None, :]
                scores.append(part.reshape(keys_count, ROWS))
            top = functools.reduce(
                jnp.maximum, [jnp.max(part, axis=0, keepdims=True) for part in scores]
            )
            weights = [jnp.exp2(part - top) for part in scores]
            total = sum(jnp.sum(part, axis=0, keepdims=True) for part in weights)
            share = 1.0 / total
            weights = [part * share for part in weights]
            probs = [part.astype(jnp.bfloat16) for part in weights]
            out = sum(dot_tn(probs[fr], vs[fr]) for fr in range(3)).astype(jnp.bfloat16)
            o_b[j, WT * band : WT * band + WT] = out.reshape(WT, TILE, HD)
            product = g.astype(jnp.float32) * out.astype(jnp.float32)
            deltas = jnp.sum(product.T, axis=0, keepdims=True)
            grads = []
            for fr in range(3):
                grad_prob = dot_nt(vs[fr], g)
                grads.append((weights[fr] * ((grad_prob - deltas) * scaling)).astype(jnp.bfloat16))
            dq = sum(dot_tn(grads[fr], ks[fr]) for fr in range(3)).astype(jnp.bfloat16)
            dq_b[j, WT * band : WT * band + WT] = dq.reshape(WT, TILE, HD)
            old = ROWS * (min(BANDS, band + 1) if band > 0 else 0)
            for fr in range(3):
                for acc, own, left, right in ((acc_k, own_k, grads, q), (acc_v, own_v, probs, g)):
                    into = own.at[j] if fr == 1 else acc.at[fr // 2]
                    part = dot_nn(left[fr], right)
                    seen = max(0, old - low * ROWS)
                    if seen:
                        into[low * ROWS : low * ROWS + seen, :] += part[:seen]
                    if seen < keys_count:
                        into[low * ROWS + seen : high * ROWS, :] = part[seen:]
        for side in range(2):
            send_k[j, side] = acc_k[side].astype(jnp.bfloat16).reshape(TILES, TILE, HD)
            send_v[j, side] = acc_v[side].astype(jnp.bfloat16).reshape(TILES, TILE, HD)

    def finish(j):
        for own, back, out in ((own_k, back_k, dk_b), (own_v, back_v, dv_b)):
            full = own[j].reshape(TILES, TILE, HD) + back[j, 0].astype(jnp.float32)
            out[j] = (full + back[j, 1].astype(jnp.float32)).astype(jnp.bfloat16)

    def share_out(j, carry):
        @pl.when(j < mine)
        def _():
            wait_in((0, 1), j)
            start_sides(HALO, j)

        @pl.when((j >= LAG) & (j - LAG < mine))
        def _():
            pass_on(HALO, j - LAG, relay_start)

        @pl.when(j < most)
        def _():
            start_in((2, 3), j)

        return carry

    lax.fori_loop(0, most, share_out, 0)

    def attend(j, carry):
        @pl.when(j < mine)
        def _():
            wait_in((2, 3), j)
            wait_sides(HALO, j)
            compute(j)
            start_sides(RET, j)
            start_out((0, 1), j)

        rest = j + most - LAG

        @pl.when(rest < mine)
        def _():
            pass_on(HALO, rest, relay_start)

        @pl.when((j >= LATER) & (j - LATER < mine))
        def _():
            pass_on(RET, j - LATER, relay_start)

        return carry

    lax.fori_loop(0, most + LATER, attend, 0)

    def gather(j, carry):
        wait_sides(RET, j)
        finish(j)
        start_out((2, 3), j)
        return carry

    lax.fori_loop(0, mine, gather, 0)

    for n in range(3):
        bias_copy(n).wait_send()

    def drain(j, carry):
        for n in range(3):
            @pl.when(j < head_count(peers[n]))
            def _():
                for arr in range(4):
                    in_copy(arr, j, n).wait_send()
                    out_copy(arr, j, n).wait_recv()

        @pl.when(j < mine)
        def _():
            for arr in range(4):
                out_own(arr, j).wait()
                for n in range(3):
                    out_copy(arr, j, n).wait_send()
            for side in range(2):
                @pl.when(has[side])
                def _():
                    for arr in range(2):
                        side_copy(HALO, arr, j, side).wait_send()
                        side_copy(RET, arr, j, side).wait_send()
            pass_on(HALO, j, relay_end)
            pass_on(RET, j, relay_end)

        return carry

    lax.fori_loop(0, most, drain, 0)


def copy_kernel(*refs):
    held, sems = refs[-2:]
    count = len(refs) // 2 - 1
    parts = [(i, t) for i in range(count) for t in range(WT)]
    loads = [pltpu.make_async_copy(refs[i].at[0, 0, t], held.at[i, t], sems.at[0, i, t]) for i, t in parts]
    stores = [pltpu.make_async_copy(held.at[i, t], refs[count + i].at[0, 0, t], sems.at[1, i, t]) for i, t in parts]
    for load in loads:
        load.start()
    for load, store in zip(loads, stores):
        load.wait()
        store.start()
    for store in stores:
        store.wait()


def on_device(frames, queries, keys, values, grad_out, windows):
    heads = queries.shape[-1] // HD
    most = (heads // 2 + 1) // 2
    near = (most, TILES, TILE, HD)
    wide = (most, 3, TILES, TILE, HD)
    both = (most, 2, TILES, TILE, HD)
    bf16 = functools.partial(pltpu.VMEM, dtype=jnp.bfloat16)
    f32 = functools.partial(pltpu.VMEM, dtype=jnp.float32)
    rows = TILES * TILE
    dma = pltpu.SemaphoreType.DMA
    anywhere = pl.BlockSpec(memory_space=pl.ANY)
    results = pl.pallas_call(
        functools.partial(kernel, frames, heads),
        name="window_attention",
        out_shape=[jax.ShapeDtypeStruct(queries.shape, jnp.bfloat16)] * 4,
        in_specs=[pl.BlockSpec(memory_space=pltpu.SMEM)] + [anywhere] * 4,
        out_specs=[anywhere] * 4,
        scratch_shapes=[
            bf16(near), bf16(near), bf16(wide), bf16(wide), f32((BANDS, 3 * TILES, ROWS)),
            f32((most, rows, HD)), f32((most, rows, HD)), f32((2, rows, HD)), f32((2, rows, HD)),
            bf16(both), bf16(both), bf16(both), bf16(both),
            bf16(near), bf16(near), bf16(near), bf16(near),
            dma((4, most, 3)), dma((4, most, 3)), dma((4, most)),
            dma((2, most, 2)), dma((2, most, 2)), dma((2, most, 2)), dma((2, most, 2)),
            dma((4, most, 3)), dma((4, most, 3)), dma((4, most)), dma((3,)), dma((3,)),
            bf16((2, 2, most, 2, TILES, TILE, HD)), dma((2, 2, most, 2)), dma((2, 2, most, 2)),
        ],
        cost_estimate=pl.CostEstimate(flops=8 * 10**9, bytes_accessed=8 * 10**6, transcendentals=4 * 10**6),
        compiler_params=pltpu.CompilerParams(
            collective_id=0, has_side_effects=True, vmem_limit_bytes=56 * 2**20
        ),
    )(windows, queries, keys, values, grad_out)
    return pl.pallas_call(
        copy_kernel,
        name="copy_out",
        out_shape=[jax.ShapeDtypeStruct(queries.shape, jnp.bfloat16)] * 4,
        in_specs=[anywhere] * 4,
        out_specs=[anywhere] * 4,
        scratch_shapes=[bf16((4, *queries.shape[2:])), dma((2, 4, WT))],
    )(*results)


def solution(mesh):
    placed = P("frame", "band", None, None, None)
    return jax.shard_map(
        functools.partial(on_device, mesh.shape["frame"]),
        mesh=mesh,
        in_specs=(placed, placed, placed, placed, P("frame", "band", None, None)),
        out_specs=(placed, placed, placed, placed),
        check_vma=False,
    )
```

```python
import functools

import jax
import jax.numpy as jnp
from jax import lax
from jax.experimental import pallas as pl
from jax.experimental.pallas import tpu as pltpu
from jax.sharding import PartitionSpec as P

MESH = pl.DeviceIdType.MESH
HD = 128
TILE = 64
WT = 2
BANDS = 4
TILES = BANDS * WT
ROWS = WT * TILE
MASKED = -1e30
AHEAD = 4
HALO, RET = 0, 1


def dot_nt(a, b):
    return lax.dot_general(a, b, (((1,), (1,)), ((), ())), preferred_element_type=jnp.float32)


def dot_tn(a, b):
    return lax.dot_general(a, b, (((0,), (0,)), ((), ())), preferred_element_type=jnp.float32)


def dot_nn(a, b):
    return jnp.dot(a, b, preferred_element_type=jnp.float32)


def kernel(
    frames, heads,
    win_ref, q_in, k_in, v_in, g_in,
    o_out, dq_out, dk_out, dv_out,
    qb, gb, kb, vb, bias, own_k, own_v, acc_k, acc_v, send_k, send_v, back_k, back_v, o_b, dq_b, dk_b, dv_b,
    in_send, in_recv, in_local, halo_send, halo_recv, ret_send, ret_recv, out_send, out_recv, out_local, bias_send, bias_recv,
    bias_own,
):
    chip_heads = heads // 2
    most = (chip_heads + 1) // 2
    half = frames // 2
    f, b = lax.axis_index("frame"), lax.axis_index("band")
    x, i, c = 2 * (b // 2) + f // half, f % half, b % 2
    p = i + half * c
    has_prev, has_next = p > 0, p < frames - 1
    last = most - 1

    def device(x, i, c):
        return half * (x % 2) + i, 2 * (x // 2) + c

    def head_count(those, at_half):
        return most - (those + at_half) % 2

    def columns(those, j):
        head = chip_heads * (those // 2) + most * (those % 2) * (1 - j // last) + j
        return pl.ds(pl.multiple_of(head * HD, HD), HD)

    def tiles(band):
        return pl.ds(WT * band, WT)

    def holder(band):
        return device(2 * (band // 2) + c, i, band % 2)

    def attender(those):
        return device(those, i, x % 2)

    def self_holds(band):
        return (band % 2 == c) & (2 * (band // 2) + c == x)

    def self_attends(those):
        return (those == x) & (x % 2 == c)

    mine = head_count(x, c)
    in_refs = (k_in, v_in, q_in, g_in)
    out_refs = (o_out, dq_out, dk_out, dv_out)
    out_bufs = (o_b, dq_b, dk_b, dv_b)

    def landing(arr, j, band):
        return (kb.at[j, 1], vb.at[j, 1], qb.at[j], gb.at[j])[arr].at[tiles(band)]

    def in_copy(arr, j, those):
        return pltpu.make_async_remote_copy(
            src_ref=in_refs[arr].at[0, 0, :, :, columns(those, j)],
            dst_ref=landing(arr, j, b),
            send_sem=in_send.at[arr, j, those],
            recv_sem=in_recv.at[arr, j, b],
            device_id=attender(those),
            device_id_type=MESH,
        )

    def in_arrival(arr, j, band):
        return pltpu.make_async_remote_copy(
            src_ref=in_refs[arr].at[0, 0, :, :, columns(x, j)],
            dst_ref=landing(arr, j, band),
            send_sem=in_send.at[arr, j, x],
            recv_sem=in_recv.at[arr, j, band],
            device_id=holder(band),
            device_id_type=MESH,
        )

    def in_own(arr, j):
        return pltpu.make_async_copy(
            in_refs[arr].at[0, 0, :, :, columns(x, j)], landing(arr, j, b), in_local.at[arr, j]
        )

    def start_in(arrs, j):
        for n in range(4):
            those = (x + 2 + n) % 4

            @pl.when((j < head_count(those, x % 2)) & jnp.logical_not(self_attends(those)))
            def _():
                for arr in arrs:
                    in_copy(arr, j, those).start()

            @pl.when((j < head_count(those, x % 2)) & self_attends(those))
            def _():
                for arr in arrs:
                    in_own(arr, j).start()

    def wait_in(arrs, j, band):
        @pl.when(self_holds(band))
        def _():
            for arr in arrs:
                in_own(arr, j).wait()

        @pl.when(jnp.logical_not(self_holds(band)))
        def _():
            for arr in arrs:
                in_arrival(arr, j, band).wait_recv()

    def to_side(side, j):
        other = p - 1 + 2 * side
        between = (other // half - c) * (other // half - c)
        beside = between * (j // last) * (1 - 2 * (x % 2))
        return device(x + beside, other % half, other // half)

    def side_refs(kind, arr, j, side):
        if kind == HALO:
            buf = (kb, vb)[arr]
            return buf.at[j, 1], buf.at[j, 2 - 2 * side], halo_send.at[arr, j, side], halo_recv.at[arr, j, side]
        return (
            (send_k, send_v)[arr].at[j, side],
            (back_k, back_v)[arr].at[j, 1 - side],
            ret_send.at[arr, j, side],
            ret_recv.at[arr, j, side],
        )

    def piece(kind, arr, j, side, n):
        source, target, send, recv = side_refs(kind, arr, j, side)
        part = tiles(n) if kind == HALO else pl.ds(2 * WT * n, 2 * WT)
        return pltpu.make_async_remote_copy(
            src_ref=source.at[part], dst_ref=target.at[part], send_sem=send.at[n], recv_sem=recv.at[n],
            device_id=to_side(side, j), device_id_type=MESH,
        )

    has = (has_prev, has_next)

    def start_pieces(kind, j, n):
        for side in range(2):
            @pl.when(has[side])
            def _():
                for arr in range(2):
                    piece(kind, arr, j, side, n).start()

    def wait_pieces(kind, j, n):
        for side in range(2):
            @pl.when(has[1 - side])
            def _():
                for arr in range(2):
                    piece(kind, arr, j, side, n).wait_recv()

    def out_copy(arr, j, band):
        return pltpu.make_async_remote_copy(
            src_ref=out_bufs[arr].at[j, tiles(band)],
            dst_ref=out_refs[arr].at[0, 0, :, :, columns(x, j)],
            send_sem=out_send.at[arr, j, band],
            recv_sem=out_recv.at[arr, j, x],
            device_id=holder(band),
            device_id_type=MESH,
        )

    def out_arrival(arr, j, those):
        return pltpu.make_async_remote_copy(
            src_ref=out_bufs[arr].at[j, tiles(b)],
            dst_ref=out_refs[arr].at[0, 0, :, :, columns(those, j)],
            send_sem=out_send.at[arr, j, b],
            recv_sem=out_recv.at[arr, j, those],
            device_id=attender(those),
            device_id_type=MESH,
        )

    def out_own(arr, j):
        return pltpu.make_async_copy(
            out_bufs[arr].at[j, tiles(b)], out_refs[arr].at[0, 0, :, :, columns(x, j)], out_local.at[arr, j]
        )

    def start_out(arrs, j, bands):
        for band in bands:
            @pl.when(self_holds(band))
            def _():
                for arr in arrs:
                    out_own(arr, j).start()

            @pl.when(jnp.logical_not(self_holds(band)))
            def _():
                for arr in arrs:
                    out_copy(arr, j, band).start()

    def bias_copy(those):
        return pltpu.make_async_remote_copy(
            src_ref=bias_own,
            dst_ref=bias.at[b],
            send_sem=bias_send.at[those],
            recv_sem=bias_recv.at[b],
            device_id=attender(those),
            device_id_type=MESH,
        )

    def bias_arrival(band):
        return pltpu.make_async_remote_copy(
            src_ref=bias_own,
            dst_ref=bias.at[band],
            send_sem=bias_send.at[x],
            recv_sem=bias_recv.at[band],
            device_id=holder(band),
            device_id_type=MESH,
        )

    middle = ((p == half - 1) | (p == half)) & (frames > 2)
    barrier = pltpu.get_barrier_semaphore()
    for step in range(1, 8):
        place = (2 * x + c + step) % 8
        pl.semaphore_signal(barrier, inc=1, device_id=device(place // 2, i, place % 2), device_id_type=MESH)
    for side in range(2):
        @pl.when(has[side])
        def _():
            pl.semaphore_signal(barrier, inc=1, device_id=to_side(side, 0), device_id_type=MESH)

        @pl.when(p == half - side)
        def _():
            pl.semaphore_signal(barrier, inc=1, device_id=to_side(side, last), device_id_type=MESH)

    place = lax.broadcasted_iota(jnp.int32, (3 * TILES, ROWS), 0) + TILES * (f - 1)
    lane = lax.broadcasted_iota(jnp.int32, (3 * TILES, ROWS), 1)
    named = []
    for t in range(WT):
        hits = [jnp.where(place == win_ref[0, 0, t, slot], 1, 0) for slot in range(8)]
        named.append(functools.reduce(jnp.maximum, hits))
    named = jnp.where(lane < TILE, named[0], named[1])
    bias_own[...] = jnp.where(named == 1, 0.0, MASKED)

    edge = jnp.logical_not(has_prev & has_next)

    @pl.when(middle)
    def _():
        pl.semaphore_wait(barrier, 10)

    @pl.when(edge)
    def _():
        pl.semaphore_wait(barrier, 8)

    @pl.when(jnp.logical_not(middle | edge))
    def _():
        pl.semaphore_wait(barrier, 9)

    start_in((0, 1), 0)
    for n in range(4):
        @pl.when(jnp.logical_not(self_attends(n)))
        def _():
            bias_copy(n).start()

        @pl.when(self_attends(n))
        def _():
            bias[b] = bias_own[...]

    lax.fori_loop(1, most, lambda j, carry: (start_in((0, 1), j), carry)[1], 0)

    nothing = jnp.zeros((most, TILES, TILE, HD), jnp.bfloat16)
    for side in range(2):
        @pl.when(jnp.logical_not(has[side]))
        def _():
            kb[:, 2 * side] = nothing
            vb[:, 2 * side] = nothing
            back_k[:, side] = nothing
            back_v[:, side] = nothing

    for n in range(4):
        @pl.when(jnp.logical_not(self_holds(n)))
        def _():
            bias_arrival(n).wait_recv()

    scaling = HD**-0.5
    scaling2 = scaling * 1.4426950408889634

    def compute(j):
        for band in range(BANDS):
            low, high = max(0, band - 1), min(BANDS, band + 2)
            tile_count = WT * (high - low)
            keys_count = tile_count * TILE
            q = qb[j, WT * band : WT * band + WT].reshape(ROWS, HD)
            g = gb[j, WT * band : WT * band + WT].reshape(ROWS, HD)
            ks = [kb[j, fr, WT * low : WT * high].reshape(keys_count, HD) for fr in range(3)]
            vs = [vb[j, fr, WT * low : WT * high].reshape(keys_count, HD) for fr in range(3)]
            scores = []
            for fr in range(3):
                start = fr * TILES + WT * low
                part = (dot_nt(ks[fr], q) * scaling2).reshape(tile_count, TILE, ROWS)
                part = part + bias[band, start : start + tile_count][:, None, :]
                scores.append(part.reshape(keys_count, ROWS))
            top = functools.reduce(
                jnp.maximum, [jnp.max(part, axis=0, keepdims=True) for part in scores]
            )
            weights = [jnp.exp2(part - top) for part in scores]
            total = sum(jnp.sum(part, axis=0, keepdims=True) for part in weights)
            share = 1.0 / total
            weights = [part * share for part in weights]
            probs = [part.astype(jnp.bfloat16) for part in weights]
            out = sum(dot_tn(probs[fr], vs[fr]) for fr in range(3)).astype(jnp.bfloat16)
            o_b[j, WT * band : WT * band + WT] = out.reshape(WT, TILE, HD)
            product = g.astype(jnp.float32) * out.astype(jnp.float32)
            deltas = jnp.sum(product.T, axis=0, keepdims=True)
            grads = []
            for fr in range(3):
                grad_prob = dot_nt(vs[fr], g)
                grads.append((weights[fr] * ((grad_prob - deltas) * scaling)).astype(jnp.bfloat16))
            dq = sum(dot_tn(grads[fr], ks[fr]) for fr in range(3)).astype(jnp.bfloat16)
            dq_b[j, WT * band : WT * band + WT] = dq.reshape(WT, TILE, HD)
            old = ROWS * (min(BANDS, band + 1) if band > 0 else 0)
            for fr in range(3):
                for acc, own, left, right in ((acc_k, own_k, grads, q), (acc_v, own_v, probs, g)):
                    into = own.at[j] if fr == 1 else acc.at[fr // 2]
                    part = dot_nn(left[fr], right)
                    seen = max(0, old - low * ROWS)
                    if seen:
                        into[low * ROWS : low * ROWS + seen, :] += part[:seen]
                    if seen < keys_count:
                        into[low * ROWS + seen : high * ROWS, :] = part[seen:]
        for side in range(2):
            send_k[j, side] = acc_k[side].astype(jnp.bfloat16).reshape(TILES, TILE, HD)
            send_v[j, side] = acc_v[side].astype(jnp.bfloat16).reshape(TILES, TILE, HD)

    def finish(j, half):
        part = pl.ds(2 * WT * half, 2 * WT)
        rows = pl.ds(pl.multiple_of(2 * ROWS * half, 2 * ROWS), 2 * ROWS)
        for own, back, out in ((own_k, back_k, dk_b), (own_v, back_v, dv_b)):
            full = own[j, rows].reshape(2 * WT, TILE, HD) + back[j, 0, part].astype(jnp.float32)
            out[j, part] = (full + back[j, 1, part].astype(jnp.float32)).astype(jnp.bfloat16)

    def share_out(j, carry):
        @pl.when(j < mine)
        def _():
            for n in range(BANDS):
                band = (2 * (x // 2) + n) % BANDS
                wait_in((0, 1), j, band)
                start_pieces(HALO, j, band)

        start_in((2, 3), j)
        return carry

    lax.fori_loop(0, most, share_out, 0)

    def attend(j, carry):
        for band in range(BANDS):
            wait_in((2, 3), j, band)
            wait_pieces(HALO, j, band)
        compute(j)
        start_pieces(RET, j, 1 - x // 2)
        start_pieces(RET, j, x // 2)
        start_out((0, 1), j, [(2 * (x // 2) + 2 + n) % BANDS for n in range(BANDS)])
        return carry

    lax.fori_loop(0, mine, attend, 0)

    def gather(j, carry):
        for part in (1 - x // 2, x // 2):
            wait_pieces(RET, j, part)
            finish(j, part)
            start_out((2, 3), j, (2 * part, 2 * part + 1))
        return carry

    lax.fori_loop(0, mine, gather, 0)

    for n in range(4):
        @pl.when(jnp.logical_not(self_attends(n)))
        def _():
            bias_copy(n).wait_send()

    def drain(j, carry):
        for n in range(4):
            @pl.when((j < head_count(n, x % 2)) & jnp.logical_not(self_attends(n)))
            def _():
                for arr in range(4):
                    in_copy(arr, j, n).wait_send()
                    out_arrival(arr, j, n).wait_recv()

            @pl.when((j < mine) & self_holds(n))
            def _():
                for arr in range(4):
                    out_own(arr, j).wait()

            @pl.when((j < mine) & jnp.logical_not(self_holds(n)))
            def _():
                for arr in range(4):
                    out_copy(arr, j, n).wait_send()

        @pl.when(j < mine)
        def _():
            for side in range(2):
                @pl.when(has[side])
                def _():
                    for arr in range(2):
                        for n in range(4):
                            piece(HALO, arr, j, side, n).wait_send()
                        for n in range(2):
                            piece(RET, arr, j, side, n).wait_send()

        return carry

    lax.fori_loop(0, most, drain, 0)


def copy_kernel(*refs):
    held, sems = refs[-2:]
    count = len(refs) // 2 - 1
    parts = [(i, t) for i in range(count) for t in range(WT)]
    loads = [pltpu.make_async_copy(refs[i].at[0, 0, t], held.at[i, t], sems.at[0, i, t]) for i, t in parts]
    stores = [pltpu.make_async_copy(held.at[i, t], refs[count + i].at[0, 0, t], sems.at[1, i, t]) for i, t in parts]
    for load in loads:
        load.start()
    for load, store in zip(loads, stores):
        load.wait()
        store.start()
    for store in stores:
        store.wait()


def on_device(frames, queries, keys, values, grad_out, windows):
    heads = queries.shape[-1] // HD
    most = (heads // 2 + 1) // 2
    near = (most, TILES, TILE, HD)
    wide = (most, 3, TILES, TILE, HD)
    both = (most, 2, TILES, TILE, HD)
    bf16 = functools.partial(pltpu.VMEM, dtype=jnp.bfloat16)
    f32 = functools.partial(pltpu.VMEM, dtype=jnp.float32)
    rows = TILES * TILE
    dma = pltpu.SemaphoreType.DMA
    anywhere = pl.BlockSpec(memory_space=pl.ANY)
    results = pl.pallas_call(
        functools.partial(kernel, frames, heads),
        name="window_attention",
        out_shape=[jax.ShapeDtypeStruct(queries.shape, jnp.bfloat16)] * 4,
        in_specs=[pl.BlockSpec(memory_space=pltpu.SMEM)] + [anywhere] * 4,
        out_specs=[anywhere] * 4,
        scratch_shapes=[
            bf16(near), bf16(near), bf16(wide), bf16(wide), f32((BANDS, 3 * TILES, ROWS)),
            f32((most, rows, HD)), f32((most, rows, HD)), f32((2, rows, HD)), f32((2, rows, HD)),
            bf16(both), bf16(both), bf16(both), bf16(both),
            bf16(near), bf16(near), bf16(near), bf16(near),
            dma((4, most, 4)), dma((4, most, 4)), dma((4, most)),
            dma((2, most, 2, 4)), dma((2, most, 2, 4)), dma((2, most, 2, 2)), dma((2, most, 2, 2)),
            dma((4, most, 4)), dma((4, most, 4)), dma((4, most)), dma((4,)), dma((4,)),
            f32((3 * TILES, ROWS)),
        ],
        cost_estimate=pl.CostEstimate(flops=8 * 10**9, bytes_accessed=8 * 10**6, transcendentals=4 * 10**6),
        compiler_params=pltpu.CompilerParams(
            collective_id=0, has_side_effects=True, vmem_limit_bytes=56 * 2**20
        ),
    )(windows, queries, keys, values, grad_out)
    return pl.pallas_call(
        copy_kernel,
        name="copy_out",
        out_shape=[jax.ShapeDtypeStruct(queries.shape, jnp.bfloat16)] * 4,
        in_specs=[anywhere] * 4,
        out_specs=[anywhere] * 4,
        scratch_shapes=[bf16((4, *queries.shape[2:])), dma((2, 4, WT))],
    )(*results)


def solution(mesh):
    placed = P("frame", "band", None, None, None)
    return jax.shard_map(
        functools.partial(on_device, mesh.shape["frame"]),
        mesh=mesh,
        in_specs=(placed, placed, placed, placed, P("frame", "band", None, None)),
        out_specs=(placed, placed, placed, placed),
        check_vma=False,
    )
```

```python
import functools

import jax
import jax.numpy as jnp
from jax import lax
from jax.experimental import pallas as pl
from jax.experimental.pallas import tpu as pltpu
from jax.sharding import PartitionSpec as P

MESH = pl.DeviceIdType.MESH
HD = 128
TILE = 64
WT = 2
BANDS = 4
TILES = BANDS * WT
ROWS = WT * TILE
MASKED = -1e30
AHEAD = 3
HALO, RET = 0, 1


def dot_nt(a, b):
    return lax.dot_general(a, b, (((1,), (1,)), ((), ())), preferred_element_type=jnp.float32)


def dot_tn(a, b):
    return lax.dot_general(a, b, (((0,), (0,)), ((), ())), preferred_element_type=jnp.float32)


def dot_nn(a, b):
    return jnp.dot(a, b, preferred_element_type=jnp.float32)


def kernel(
    frames, heads,
    win_ref, q_in, k_in, v_in, g_in,
    o_out, dq_out, dk_out, dv_out,
    qb, gb, kb, vb, bias, own_k, own_v, acc_k, acc_v, send_k, send_v, back_k, back_v, o_b, dq_b, dk_b, dv_b,
    in_send, in_recv, in_local, halo_send, halo_recv, ret_send, ret_recv, out_send, out_recv, out_local, bias_send, bias_recv,
    bias_own,
):
    chip_heads = heads // 2
    most = (chip_heads + 1) // 2
    half = frames // 2
    f, b = lax.axis_index("frame"), lax.axis_index("band")
    x, i, c = 2 * (b // 2) + f // half, f % half, b % 2
    p = i + half * c
    has_prev, has_next = p > 0, p < frames - 1
    last = most - 1

    def device(x, i, c):
        return half * (x % 2) + i, 2 * (x // 2) + c

    def head_count(those, at_half):
        return most - (those + at_half) % 2

    def columns(those, j):
        head = chip_heads * (those // 2) + most * (those % 2) * (1 - j // last) + j
        return pl.ds(pl.multiple_of(head * HD, HD), HD)

    def tiles(band):
        return pl.ds(WT * band, WT)

    def holder(band):
        return device(2 * (band // 2) + c, i, band % 2)

    def attender(those):
        return device(those, i, x % 2)

    def self_holds(band):
        return (band % 2 == c) & (2 * (band // 2) + c == x)

    def self_attends(those):
        return (those == x) & (x % 2 == c)

    mine = head_count(x, c)
    in_refs = (k_in, v_in, q_in, g_in)
    out_refs = (o_out, dq_out, dk_out, dv_out)
    out_bufs = (o_b, dq_b, dk_b, dv_b)

    def landing(arr, j, band):
        return (kb.at[j, 1], vb.at[j, 1], qb.at[j], gb.at[j])[arr].at[tiles(band)]

    def in_copy(arr, j, those):
        return pltpu.make_async_remote_copy(
            src_ref=in_refs[arr].at[0, 0, :, :, columns(those, j)],
            dst_ref=landing(arr, j, b),
            send_sem=in_send.at[arr, j, those],
            recv_sem=in_recv.at[arr, j, b],
            device_id=attender(those),
            device_id_type=MESH,
        )

    def in_arrival(arr, j, band):
        return pltpu.make_async_remote_copy(
            src_ref=in_refs[arr].at[0, 0, :, :, columns(x, j)],
            dst_ref=landing(arr, j, band),
            send_sem=in_send.at[arr, j, x],
            recv_sem=in_recv.at[arr, j, band],
            device_id=holder(band),
            device_id_type=MESH,
        )

    def in_own(arr, j):
        return pltpu.make_async_copy(
            in_refs[arr].at[0, 0, :, :, columns(x, j)], landing(arr, j, b), in_local.at[arr, j]
        )

    def start_in(arrs, j):
        for n in range(4):
            those = (x + 2 + n) % 4

            @pl.when((j < head_count(those, x % 2)) & jnp.logical_not(self_attends(those)))
            def _():
                for arr in arrs:
                    in_copy(arr, j, those).start()

            @pl.when((j < head_count(those, x % 2)) & self_attends(those))
            def _():
                for arr in arrs:
                    in_own(arr, j).start()

    def wait_in(arrs, j, band):
        @pl.when(self_holds(band))
        def _():
            for arr in arrs:
                in_own(arr, j).wait()

        @pl.when(jnp.logical_not(self_holds(band)))
        def _():
            for arr in arrs:
                in_arrival(arr, j, band).wait_recv()

    def to_side(side, j):
        other = p - 1 + 2 * side
        between = (other // half - c) * (other // half - c)
        beside = between * (j // last) * (1 - 2 * (x % 2))
        return device(x + beside, other % half, other // half)

    def side_refs(kind, arr, j, side):
        if kind == HALO:
            buf = (kb, vb)[arr]
            return buf.at[j, 1], buf.at[j, 2 - 2 * side], halo_send.at[arr, j, side], halo_recv.at[arr, j, side]
        return (
            (send_k, send_v)[arr].at[j, side],
            (back_k, back_v)[arr].at[j, 1 - side],
            ret_send.at[arr, j, side],
            ret_recv.at[arr, j, side],
        )

    def piece(kind, arr, j, side, n, straight=False):
        source, target, send, recv = side_refs(kind, arr, j, side)
        part = tiles(n) if kind == HALO else pl.ds(2 * WT * n, 2 * WT)
        source = in_refs[arr].at[0, 0, :, :, columns(x, j)] if straight else source.at[part]
        return pltpu.make_async_remote_copy(
            src_ref=source, dst_ref=target.at[part], send_sem=send.at[n], recv_sem=recv.at[n],
            device_id=to_side(side, j), device_id_type=MESH,
        )

    has = (has_prev, has_next)

    def start_pieces(kind, j, n, straight=False):
        for side in range(2):
            @pl.when(has[side])
            def _():
                for arr in range(2):
                    piece(kind, arr, j, side, n, straight).start()

    def wait_pieces(kind, j, n):
        for side in range(2):
            @pl.when(has[1 - side])
            def _():
                for arr in range(2):
                    piece(kind, arr, j, side, n).wait_recv()

    def out_copy(arr, j, band):
        return pltpu.make_async_remote_copy(
            src_ref=out_bufs[arr].at[j, tiles(band)],
            dst_ref=out_refs[arr].at[0, 0, :, :, columns(x, j)],
            send_sem=out_send.at[arr, j, band],
            recv_sem=out_recv.at[arr, j, x],
            device_id=holder(band),
            device_id_type=MESH,
        )

    def out_arrival(arr, j, those):
        return pltpu.make_async_remote_copy(
            src_ref=out_bufs[arr].at[j, tiles(b)],
            dst_ref=out_refs[arr].at[0, 0, :, :, columns(those, j)],
            send_sem=out_send.at[arr, j, b],
            recv_sem=out_recv.at[arr, j, those],
            device_id=attender(those),
            device_id_type=MESH,
        )

    def out_own(arr, j):
        return pltpu.make_async_copy(
            out_bufs[arr].at[j, tiles(b)], out_refs[arr].at[0, 0, :, :, columns(x, j)], out_local.at[arr, j]
        )

    def start_out(arrs, j, bands):
        for band in bands:
            @pl.when(self_holds(band))
            def _():
                for arr in arrs:
                    out_own(arr, j).start()

            @pl.when(jnp.logical_not(self_holds(band)))
            def _():
                for arr in arrs:
                    out_copy(arr, j, band).start()

    def bias_copy(those):
        return pltpu.make_async_remote_copy(
            src_ref=bias_own,
            dst_ref=bias.at[b],
            send_sem=bias_send.at[those],
            recv_sem=bias_recv.at[b],
            device_id=attender(those),
            device_id_type=MESH,
        )

    def bias_arrival(band):
        return pltpu.make_async_remote_copy(
            src_ref=bias_own,
            dst_ref=bias.at[band],
            send_sem=bias_send.at[x],
            recv_sem=bias_recv.at[band],
            device_id=holder(band),
            device_id_type=MESH,
        )

    middle = ((p == half - 1) | (p == half)) & (frames > 2)
    barrier = pltpu.get_barrier_semaphore()
    for step in range(1, 8):
        place = (2 * x + c + step) % 8
        pl.semaphore_signal(barrier, inc=1, device_id=device(place // 2, i, place % 2), device_id_type=MESH)
    for side in range(2):
        @pl.when(has[side])
        def _():
            pl.semaphore_signal(barrier, inc=1, device_id=to_side(side, 0), device_id_type=MESH)

        @pl.when(p == half - side)
        def _():
            pl.semaphore_signal(barrier, inc=1, device_id=to_side(side, last), device_id_type=MESH)

    place = lax.broadcasted_iota(jnp.int32, (3 * TILES, ROWS), 0) + TILES * (f - 1)
    lane = lax.broadcasted_iota(jnp.int32, (3 * TILES, ROWS), 1)
    named = []
    for t in range(WT):
        hits = [jnp.where(place == win_ref[0, 0, t, slot], 1, 0) for slot in range(8)]
        named.append(functools.reduce(jnp.maximum, hits))
    named = jnp.where(lane < TILE, named[0], named[1])
    bias_own[...] = jnp.where(named == 1, 0.0, MASKED)

    edge = jnp.logical_not(has_prev & has_next)

    @pl.when(middle)
    def _():
        pl.semaphore_wait(barrier, 10)

    @pl.when(edge)
    def _():
        pl.semaphore_wait(barrier, 8)

    @pl.when(jnp.logical_not(middle | edge))
    def _():
        pl.semaphore_wait(barrier, 9)

    start_in((0, 1), 0)

    @pl.when(x % 2 == c)
    def _():
        start_pieces(HALO, 0, b, True)
        start_pieces(HALO, 1, b, True)

    for n in range(4):
        @pl.when(jnp.logical_not(self_attends(n)))
        def _():
            bias_copy(n).start()

        @pl.when(self_attends(n))
        def _():
            bias[b] = bias_own[...]

    for j in range(1, AHEAD):
        start_in((0, 1), j)

    nothing = jnp.zeros((most, TILES, TILE, HD), jnp.bfloat16)
    for side in range(2):
        @pl.when(jnp.logical_not(has[side]))
        def _():
            kb[:, 2 * side] = nothing
            vb[:, 2 * side] = nothing
            back_k[:, side] = nothing
            back_v[:, side] = nothing

    for n in range(4):
        @pl.when(jnp.logical_not(self_holds(n)))
        def _():
            bias_arrival(n).wait_recv()

    scaling = HD**-0.5
    scaling2 = scaling * 1.4426950408889634

    def compute(j):
        for band in range(BANDS):
            low, high = max(0, band - 1), min(BANDS, band + 2)
            tile_count = WT * (high - low)
            keys_count = tile_count * TILE
            q = qb[j, WT * band : WT * band + WT].reshape(ROWS, HD)
            g = gb[j, WT * band : WT * band + WT].reshape(ROWS, HD)
            ks = [kb[j, fr, WT * low : WT * high].reshape(keys_count, HD) for fr in range(3)]
            vs = [vb[j, fr, WT * low : WT * high].reshape(keys_count, HD) for fr in range(3)]
            scores = []
            for fr in range(3):
                start = fr * TILES + WT * low
                part = (dot_nt(ks[fr], q) * scaling2).reshape(tile_count, TILE, ROWS)
                part = part + bias[band, start : start + tile_count][:, None, :]
                scores.append(part.reshape(keys_count, ROWS))
            top = functools.reduce(
                jnp.maximum, [jnp.max(part, axis=0, keepdims=True) for part in scores]
            )
            weights = [jnp.exp2(part - top) for part in scores]
            total = sum(jnp.sum(part, axis=0, keepdims=True) for part in weights)
            share = 1.0 / total
            weights = [part * share for part in weights]
            probs = [part.astype(jnp.bfloat16) for part in weights]
            out = sum(dot_tn(probs[fr], vs[fr]) for fr in range(3)).astype(jnp.bfloat16)
            o_b[j, WT * band : WT * band + WT] = out.reshape(WT, TILE, HD)
            product = g.astype(jnp.float32) * out.astype(jnp.float32)
            deltas = jnp.sum(product.T, axis=0, keepdims=True)
            grads = []
            for fr in range(3):
                grad_prob = dot_nt(vs[fr], g)
                grads.append((weights[fr] * ((grad_prob - deltas) * scaling)).astype(jnp.bfloat16))
            dq = sum(dot_tn(grads[fr], ks[fr]) for fr in range(3)).astype(jnp.bfloat16)
            dq_b[j, WT * band : WT * band + WT] = dq.reshape(WT, TILE, HD)
            old = ROWS * (min(BANDS, band + 1) if band > 0 else 0)
            for fr in range(3):
                for acc, own, left, right in ((acc_k, own_k, grads, q), (acc_v, own_v, probs, g)):
                    into = own.at[j] if fr == 1 else acc.at[fr // 2]
                    part = dot_nn(left[fr], right)
                    seen = max(0, old - low * ROWS)
                    if seen:
                        into[low * ROWS : low * ROWS + seen, :] += part[:seen]
                    if seen < keys_count:
                        into[low * ROWS + seen : high * ROWS, :] = part[seen:]
        for side in range(2):
            send_k[j, side] = acc_k[side].astype(jnp.bfloat16).reshape(TILES, TILE, HD)
            send_v[j, side] = acc_v[side].astype(jnp.bfloat16).reshape(TILES, TILE, HD)

    def finish(j, half):
        part = pl.ds(2 * WT * half, 2 * WT)
        rows = pl.ds(pl.multiple_of(2 * ROWS * half, 2 * ROWS), 2 * ROWS)
        for own, back, out in ((own_k, back_k, dk_b), (own_v, back_v, dv_b)):
            full = own[j, rows].reshape(2 * WT, TILE, HD) + back[j, 0, part].astype(jnp.float32)
            out[j, part] = (full + back[j, 1, part].astype(jnp.float32)).astype(jnp.bfloat16)

    def share_out(j, carry):
        @pl.when(j < mine)
        def _():
            for n in range(BANDS):
                band = (2 * (x // 2) + n) % BANDS
                wait_in((0, 1), j, band)

                @pl.when(jnp.logical_not(self_holds(band)))
                def _():
                    start_pieces(HALO, j, band)

        @pl.when(j + AHEAD < most)
        def _():
            start_in((0, 1), j + AHEAD)

        start_in((2, 3), j)

        @pl.when((x % 2 == c) & (j + 2 < mine))
        def _():
            start_pieces(HALO, j + 2, b, True)

        return carry

    lax.fori_loop(0, most, share_out, 0)

    def attend(j, carry):
        for band in range(BANDS):
            wait_in((2, 3), j, band)
            wait_pieces(HALO, j, band)
        compute(j)
        start_pieces(RET, j, 1 - x // 2)
        start_pieces(RET, j, x // 2)
        start_out((0, 1), j, [(2 * (x // 2) + 2 + n) % BANDS for n in range(BANDS)])
        return carry

    lax.fori_loop(0, mine, attend, 0)

    def settle(arrs, j):
        for n in range(4):
            @pl.when((j < head_count(n, x % 2)) & jnp.logical_not(self_attends(n)))
            def _():
                for arr in arrs:
                    out_arrival(arr, j, n).wait_recv()

            @pl.when((j < mine) & self_holds(n))
            def _():
                for arr in arrs:
                    out_own(arr, j).wait()

            @pl.when((j < mine) & jnp.logical_not(self_holds(n)))
            def _():
                for arr in arrs:
                    out_copy(arr, j, n).wait_send()

    def settle_sides(kind, j):
        for side in range(2):
            @pl.when((j < mine) & has[side])
            def _():
                for arr in range(2):
                    for n in range(4 if kind == HALO else 2):
                        piece(kind, arr, j, side, n).wait_send()

    def settle_in(j):
        for n in range(4):
            @pl.when((j < head_count(n, x % 2)) & jnp.logical_not(self_attends(n)))
            def _():
                for arr in range(4):
                    in_copy(arr, j, n).wait_send()

    def gather(j, carry):
        settle_in(j)
        settle_sides(HALO, j)

        @pl.when(j >= 1)
        def _():
            settle((0, 1), j - 1)

        @pl.when(j >= 2)
        def _():
            settle((2, 3), j - 2)
            settle_sides(RET, j - 2)

        @pl.when(j < mine)
        def _():
            for part in (1 - x // 2, x // 2):
                wait_pieces(RET, j, part)
                finish(j, part)
                start_out((2, 3), j, (2 * part, 2 * part + 1))

        return carry

    lax.fori_loop(0, most, gather, 0)

    for n in range(4):
        @pl.when(jnp.logical_not(self_attends(n)))
        def _():
            bias_copy(n).wait_send()

    settle((0, 1), most - 1)
    for j in (most - 2, most - 1):
        settle((2, 3), j)
        settle_sides(RET, j)


def copy_kernel(*refs):
    held, sems = refs[-2:]
    count = len(refs) // 2 - 1
    parts = [(i, t) for i in range(count) for t in range(WT)]
    loads = [pltpu.make_async_copy(refs[i].at[0, 0, t], held.at[i, t], sems.at[0, i, t]) for i, t in parts]
    stores = [pltpu.make_async_copy(held.at[i, t], refs[count + i].at[0, 0, t], sems.at[1, i, t]) for i, t in parts]
    for load in loads:
        load.start()
    for load, store in zip(loads, stores):
        load.wait()
        store.start()
    for store in stores:
        store.wait()


def on_device(frames, queries, keys, values, grad_out, windows):
    heads = queries.shape[-1] // HD
    most = (heads // 2 + 1) // 2
    near = (most, TILES, TILE, HD)
    wide = (most, 3, TILES, TILE, HD)
    both = (most, 2, TILES, TILE, HD)
    bf16 = functools.partial(pltpu.VMEM, dtype=jnp.bfloat16)
    f32 = functools.partial(pltpu.VMEM, dtype=jnp.float32)
    rows = TILES * TILE
    dma = pltpu.SemaphoreType.DMA
    anywhere = pl.BlockSpec(memory_space=pl.ANY)
    results = pl.pallas_call(
        functools.partial(kernel, frames, heads),
        name="window_attention",
        out_shape=[jax.ShapeDtypeStruct(queries.shape, jnp.bfloat16)] * 4,
        in_specs=[pl.BlockSpec(memory_space=pltpu.SMEM)] + [anywhere] * 4,
        out_specs=[anywhere] * 4,
        scratch_shapes=[
            bf16(near), bf16(near), bf16(wide), bf16(wide), f32((BANDS, 3 * TILES, ROWS)),
            f32((most, rows, HD)), f32((most, rows, HD)), f32((2, rows, HD)), f32((2, rows, HD)),
            bf16(both), bf16(both), bf16(both), bf16(both),
            bf16(near), bf16(near), bf16(near), bf16(near),
            dma((4, most, 4)), dma((4, most, 4)), dma((4, most)),
            dma((2, most, 2, 4)), dma((2, most, 2, 4)), dma((2, most, 2, 2)), dma((2, most, 2, 2)),
            dma((4, most, 4)), dma((4, most, 4)), dma((4, most)), dma((4,)), dma((4,)),
            f32((3 * TILES, ROWS)),
        ],
        cost_estimate=pl.CostEstimate(flops=8 * 10**9, bytes_accessed=8 * 10**6, transcendentals=4 * 10**6),
        compiler_params=pltpu.CompilerParams(
            collective_id=0, has_side_effects=True, vmem_limit_bytes=56 * 2**20
        ),
    )(windows, queries, keys, values, grad_out)
    return pl.pallas_call(
        copy_kernel,
        name="copy_out",
        out_shape=[jax.ShapeDtypeStruct(queries.shape, jnp.bfloat16)] * 4,
        in_specs=[anywhere] * 4,
        out_specs=[anywhere] * 4,
        scratch_shapes=[bf16((4, *queries.shape[2:])), dma((2, 4, WT))],
    )(*results)


def solution(mesh):
    placed = P("frame", "band", None, None, None)
    return jax.shard_map(
        functools.partial(on_device, mesh.shape["frame"]),
        mesh=mesh,
        in_specs=(placed, placed, placed, placed, P("frame", "band", None, None)),
        out_specs=(placed, placed, placed, placed),
        check_vma=False,
    )
```

```python
import functools

import jax
import jax.numpy as jnp
from jax import lax
from jax.experimental import pallas as pl
from jax.experimental.pallas import tpu as pltpu
from jax.sharding import PartitionSpec as P

MESH = pl.DeviceIdType.MESH
HD = 128
TILE = 64
WT = 2
BANDS = 4
TILES = BANDS * WT
ROWS = WT * TILE
MASKED = -1e30
AHEAD = 3
HALO, RET = 0, 1


def dot_nt(a, b):
    return lax.dot_general(a, b, (((1,), (1,)), ((), ())), preferred_element_type=jnp.float32)


def dot_tn(a, b):
    return lax.dot_general(a, b, (((0,), (0,)), ((), ())), preferred_element_type=jnp.float32)


def dot_nn(a, b):
    return jnp.dot(a, b, preferred_element_type=jnp.float32)


def kernel(
    frames, heads,
    win_ref, q_in, k_in, v_in, g_in,
    o_out, dq_out, dk_out, dv_out,
    qb, gb, kb, vb, bias, own_k, own_v, acc_k, acc_v, send_k, send_v, back_k, back_v, o_b, dq_b, dk_b, dv_b,
    in_send, in_recv, in_local, halo_send, halo_recv, ret_send, ret_recv, out_send, out_recv, out_local, bias_send, bias_recv,
    bias_own,
):
    chip_heads = heads // 2
    most = (chip_heads + 1) // 2
    half = frames // 2
    f, b = lax.axis_index("frame"), lax.axis_index("band")
    x, i, c = 2 * (b // 2) + f // half, f % half, b % 2
    p = i + half * c
    has_prev, has_next = p > 0, p < frames - 1
    last = most - 1

    def device(x, i, c):
        return half * (x % 2) + i, 2 * (x // 2) + c

    def head_count(those, at_half):
        return most - (those + at_half) % 2

    def columns(those, j):
        head = chip_heads * (those // 2) + most * (those % 2) * (1 - j // last) + j
        return pl.ds(pl.multiple_of(head * HD, HD), HD)

    def tiles(band):
        return pl.ds(WT * band, WT)

    def holder(band):
        return device(2 * (band // 2) + c, i, band % 2)

    def attender(those):
        return device(those, i, x % 2)

    def self_holds(band):
        return (band % 2 == c) & (2 * (band // 2) + c == x)

    def self_attends(those):
        return (those == x) & (x % 2 == c)

    mine = head_count(x, c)
    in_refs = (k_in, v_in, q_in, g_in)
    out_refs = (o_out, dq_out, dk_out, dv_out)
    out_bufs = (o_b, dq_b, dk_b, dv_b)

    def landing(arr, j, band):
        return (kb.at[j, 1], vb.at[j, 1], qb.at[j], gb.at[j])[arr].at[tiles(band)]

    def in_copy(arr, j, those):
        return pltpu.make_async_remote_copy(
            src_ref=in_refs[arr].at[0, 0, :, :, columns(those, j)],
            dst_ref=landing(arr, j, b),
            send_sem=in_send.at[arr, j, those],
            recv_sem=in_recv.at[arr, j, b],
            device_id=attender(those),
            device_id_type=MESH,
        )

    def in_arrival(arr, j, band):
        return pltpu.make_async_remote_copy(
            src_ref=in_refs[arr].at[0, 0, :, :, columns(x, j)],
            dst_ref=landing(arr, j, band),
            send_sem=in_send.at[arr, j, x],
            recv_sem=in_recv.at[arr, j, band],
            device_id=holder(band),
            device_id_type=MESH,
        )

    def in_own(arr, j):
        return pltpu.make_async_copy(
            in_refs[arr].at[0, 0, :, :, columns(x, j)], landing(arr, j, b), in_local.at[arr, j]
        )

    def start_in(arrs, j):
        for n in range(4):
            those = (x + 2 + n) % 4

            @pl.when((j < head_count(those, x % 2)) & jnp.logical_not(self_attends(those)))
            def _():
                for arr in arrs:
                    in_copy(arr, j, those).start()

            @pl.when((j < head_count(those, x % 2)) & self_attends(those))
            def _():
                for arr in arrs:
                    in_own(arr, j).start()

    def wait_in(arrs, j, band):
        @pl.when(self_holds(band))
        def _():
            for arr in arrs:
                in_own(arr, j).wait()

        @pl.when(jnp.logical_not(self_holds(band)))
        def _():
            for arr in arrs:
                in_arrival(arr, j, band).wait_recv()

    def to_side(side, j):
        other = p - 1 + 2 * side
        between = (other // half - c) * (other // half - c)
        beside = between * (j // last) * (1 - 2 * (x % 2))
        return device(x + beside, other % half, other // half)

    def side_refs(kind, arr, j, side):
        if kind == HALO:
            buf = (kb, vb)[arr]
            return buf.at[j, 1], buf.at[j, 2 - 2 * side], halo_send.at[arr, j, side], halo_recv.at[arr, j, side]
        return (
            (send_k, send_v)[arr].at[j, side],
            (back_k, back_v)[arr].at[j, 1 - side],
            ret_send.at[arr, j, side],
            ret_recv.at[arr, j, side],
        )

    def piece(kind, arr, j, side, n, straight=False):
        source, target, send, recv = side_refs(kind, arr, j, side)
        part = tiles(n) if kind == HALO else pl.ds(2 * WT * n, 2 * WT)
        source = in_refs[arr].at[0, 0, :, :, columns(x, j)] if straight else source.at[part]
        return pltpu.make_async_remote_copy(
            src_ref=source, dst_ref=target.at[part], send_sem=send.at[n], recv_sem=recv.at[n],
            device_id=to_side(side, j), device_id_type=MESH,
        )

    has = (has_prev, has_next)

    def start_pieces(kind, j, n, straight=False):
        for side in range(2):
            @pl.when(has[side])
            def _():
                for arr in range(2):
                    piece(kind, arr, j, side, n, straight).start()

    def wait_pieces(kind, j, n):
        for side in range(2):
            @pl.when(has[1 - side])
            def _():
                for arr in range(2):
                    piece(kind, arr, j, side, n).wait_recv()

    def out_copy(arr, j, band):
        return pltpu.make_async_remote_copy(
            src_ref=out_bufs[arr].at[j, tiles(band)],
            dst_ref=out_refs[arr].at[0, 0, :, :, columns(x, j)],
            send_sem=out_send.at[arr, j, band],
            recv_sem=out_recv.at[arr, j, x],
            device_id=holder(band),
            device_id_type=MESH,
        )

    def out_arrival(arr, j, those):
        return pltpu.make_async_remote_copy(
            src_ref=out_bufs[arr].at[j, tiles(b)],
            dst_ref=out_refs[arr].at[0, 0, :, :, columns(those, j)],
            send_sem=out_send.at[arr, j, b],
            recv_sem=out_recv.at[arr, j, those],
            device_id=attender(those),
            device_id_type=MESH,
        )

    def out_own(arr, j):
        return pltpu.make_async_copy(
            out_bufs[arr].at[j, tiles(b)], out_refs[arr].at[0, 0, :, :, columns(x, j)], out_local.at[arr, j]
        )

    def start_out(arrs, j, bands):
        for band in bands:
            @pl.when(self_holds(band))
            def _():
                for arr in arrs:
                    out_own(arr, j).start()

            @pl.when(jnp.logical_not(self_holds(band)))
            def _():
                for arr in arrs:
                    out_copy(arr, j, band).start()

    def bias_copy(those):
        return pltpu.make_async_remote_copy(
            src_ref=bias_own,
            dst_ref=bias.at[b],
            send_sem=bias_send.at[those],
            recv_sem=bias_recv.at[b],
            device_id=attender(those),
            device_id_type=MESH,
        )

    def bias_arrival(band):
        return pltpu.make_async_remote_copy(
            src_ref=bias_own,
            dst_ref=bias.at[band],
            send_sem=bias_send.at[x],
            recv_sem=bias_recv.at[band],
            device_id=holder(band),
            device_id_type=MESH,
        )

    middle = ((p == half - 1) | (p == half)) & (frames > 2)
    barrier = pltpu.get_barrier_semaphore()
    for step in range(1, 8):
        place = (2 * x + c + step) % 8
        pl.semaphore_signal(barrier, inc=1, device_id=device(place // 2, i, place % 2), device_id_type=MESH)
    for side in range(2):
        @pl.when(has[side])
        def _():
            pl.semaphore_signal(barrier, inc=1, device_id=to_side(side, 0), device_id_type=MESH)

        @pl.when(p == half - side)
        def _():
            pl.semaphore_signal(barrier, inc=1, device_id=to_side(side, last), device_id_type=MESH)

    place = lax.broadcasted_iota(jnp.int32, (3 * TILES, ROWS), 0) + TILES * (f - 1)
    lane = lax.broadcasted_iota(jnp.int32, (3 * TILES, ROWS), 1)
    named = []
    for t in range(WT):
        hits = [jnp.where(place == win_ref[0, 0, t, slot], 1, 0) for slot in range(8)]
        named.append(functools.reduce(jnp.maximum, hits))
    named = jnp.where(lane < TILE, named[0], named[1])
    bias_own[...] = jnp.where(named == 1, 0.0, MASKED)

    edge = jnp.logical_not(has_prev & has_next)

    @pl.when(middle)
    def _():
        pl.semaphore_wait(barrier, 10)

    @pl.when(edge)
    def _():
        pl.semaphore_wait(barrier, 8)

    @pl.when(jnp.logical_not(middle | edge))
    def _():
        pl.semaphore_wait(barrier, 9)

    @pl.when(x % 2 == c)
    def _():
        start_pieces(HALO, 0, b, True)

    start_in((0, 1), 0)

    @pl.when(x % 2 == c)
    def _():
        start_pieces(HALO, 1, b, True)
        start_pieces(HALO, 2, b, True)

    for n in range(4):
        @pl.when(jnp.logical_not(self_attends(n)))
        def _():
            bias_copy(n).start()

        @pl.when(self_attends(n))
        def _():
            bias[b] = bias_own[...]

    for j in range(1, AHEAD):
        start_in((0, 1), j)

    nothing = jnp.zeros((most, TILES, TILE, HD), jnp.bfloat16)
    for side in range(2):
        @pl.when(jnp.logical_not(has[side]))
        def _():
            kb[:, 2 * side] = nothing
            vb[:, 2 * side] = nothing
            back_k[:, side] = nothing
            back_v[:, side] = nothing

    for n in range(4):
        @pl.when(jnp.logical_not(self_holds(n)))
        def _():
            bias_arrival(n).wait_recv()

    scaling = HD**-0.5
    scaling2 = scaling * 1.4426950408889634

    def compute(j):
        for band in range(BANDS):
            low, high = max(0, band - 1), min(BANDS, band + 2)
            tile_count = WT * (high - low)
            keys_count = tile_count * TILE
            q = qb[j, WT * band : WT * band + WT].reshape(ROWS, HD)
            g = gb[j, WT * band : WT * band + WT].reshape(ROWS, HD)
            ks = [kb[j, fr, WT * low : WT * high].reshape(keys_count, HD) for fr in range(3)]
            vs = [vb[j, fr, WT * low : WT * high].reshape(keys_count, HD) for fr in range(3)]
            scores = []
            for fr in range(3):
                start = fr * TILES + WT * low
                part = (dot_nt(ks[fr], q) * scaling2).reshape(tile_count, TILE, ROWS)
                part = part + bias[band, start : start + tile_count][:, None, :]
                scores.append(part.reshape(keys_count, ROWS))
            top = functools.reduce(
                jnp.maximum, [jnp.max(part, axis=0, keepdims=True) for part in scores]
            )
            weights = [jnp.exp2(part - top) for part in scores]
            total = sum(jnp.sum(part, axis=0, keepdims=True) for part in weights)
            share = 1.0 / total
            weights = [part * share for part in weights]
            probs = [part.astype(jnp.bfloat16) for part in weights]
            out = sum(dot_tn(probs[fr], vs[fr]) for fr in range(3)).astype(jnp.bfloat16)
            o_b[j, WT * band : WT * band + WT] = out.reshape(WT, TILE, HD)
            product = g.astype(jnp.float32) * out.astype(jnp.float32)
            deltas = jnp.sum(product.T, axis=0, keepdims=True)
            grads = []
            for fr in range(3):
                grad_prob = dot_nt(vs[fr], g)
                grads.append((weights[fr] * ((grad_prob - deltas) * scaling)).astype(jnp.bfloat16))
            dq = sum(dot_tn(grads[fr], ks[fr]) for fr in range(3)).astype(jnp.bfloat16)
            dq_b[j, WT * band : WT * band + WT] = dq.reshape(WT, TILE, HD)
            old = ROWS * (min(BANDS, band + 1) if band > 0 else 0)
            for fr in range(3):
                for acc, own, left, right in ((acc_k, own_k, grads, q), (acc_v, own_v, probs, g)):
                    into = own.at[j] if fr == 1 else acc.at[fr // 2]
                    part = dot_nn(left[fr], right)
                    seen = max(0, old - low * ROWS)
                    if seen:
                        into[low * ROWS : low * ROWS + seen, :] += part[:seen]
                    if seen < keys_count:
                        into[low * ROWS + seen : high * ROWS, :] = part[seen:]
        for side in range(2):
            send_k[j, side] = acc_k[side].astype(jnp.bfloat16).reshape(TILES, TILE, HD)
            send_v[j, side] = acc_v[side].astype(jnp.bfloat16).reshape(TILES, TILE, HD)

    def finish(j, half):
        part = pl.ds(2 * WT * half, 2 * WT)
        rows = pl.ds(pl.multiple_of(2 * ROWS * half, 2 * ROWS), 2 * ROWS)
        for own, back, out in ((own_k, back_k, dk_b), (own_v, back_v, dv_b)):
            full = own[j, rows].reshape(2 * WT, TILE, HD) + back[j, 0, part].astype(jnp.float32)
            out[j, part] = (full + back[j, 1, part].astype(jnp.float32)).astype(jnp.bfloat16)

    def share_out(j, carry):
        @pl.when(j < mine)
        def _():
            for n in range(BANDS):
                band = (2 * (x // 2) + n) % BANDS
                wait_in((0, 1), j, band)

                @pl.when(jnp.logical_not(self_holds(band)))
                def _():
                    start_pieces(HALO, j, band)

        @pl.when(j + AHEAD < most)
        def _():
            start_in((0, 1), j + AHEAD)

        start_in((2, 3), j)

        @pl.when((x % 2 == c) & (j + 3 < mine))
        def _():
            start_pieces(HALO, j + 3, b, True)

        return carry

    lax.fori_loop(0, most, share_out, 0)

    def attend(j, carry):
        for band in range(BANDS):
            wait_in((2, 3), j, band)
            wait_pieces(HALO, j, band)
        compute(j)
        start_pieces(RET, j, 1 - x // 2)
        start_pieces(RET, j, x // 2)
        start_out((0, 1), j, [(2 * (x // 2) + 2 + n) % BANDS for n in range(BANDS)])
        return carry

    lax.fori_loop(0, mine, attend, 0)

    def settle(arrs, j):
        for n in range(4):
            @pl.when((j < head_count(n, x % 2)) & jnp.logical_not(self_attends(n)))
            def _():
                for arr in arrs:
                    out_arrival(arr, j, n).wait_recv()

            @pl.when((j < mine) & self_holds(n))
            def _():
                for arr in arrs:
                    out_own(arr, j).wait()

            @pl.when((j < mine) & jnp.logical_not(self_holds(n)))
            def _():
                for arr in arrs:
                    out_copy(arr, j, n).wait_send()

    def settle_sides(kind, j):
        for side in range(2):
            @pl.when((j < mine) & has[side])
            def _():
                for arr in range(2):
                    for n in range(4 if kind == HALO else 2):
                        piece(kind, arr, j, side, n).wait_send()

    def settle_in(j):
        for n in range(4):
            @pl.when((j < head_count(n, x % 2)) & jnp.logical_not(self_attends(n)))
            def _():
                for arr in range(4):
                    in_copy(arr, j, n).wait_send()

    def gather(j, carry):
        settle_in(j)
        settle_sides(HALO, j)

        @pl.when(j >= 1)
        def _():
            settle((0, 1), j - 1)

        @pl.when(j >= 2)
        def _():
            settle((2, 3), j - 2)
            settle_sides(RET, j - 2)

        @pl.when(j < mine)
        def _():
            for part in (1 - x // 2, x // 2):
                wait_pieces(RET, j, part)
                finish(j, part)
                start_out((2, 3), j, (2 * part, 2 * part + 1))

        return carry

    lax.fori_loop(0, most, gather, 0)

    for n in range(4):
        @pl.when(jnp.logical_not(self_attends(n)))
        def _():
            bias_copy(n).wait_send()

    settle((0, 1), most - 1)
    for j in (most - 2, most - 1):
        settle((2, 3), j)
        settle_sides(RET, j)


def copy_kernel(*refs):
    held, sems = refs[-2:]
    count = len(refs) // 2 - 1
    parts = [(i, t) for i in range(count) for t in range(WT)]
    loads = [pltpu.make_async_copy(refs[i].at[0, 0, t], held.at[i, t], sems.at[0, i, t]) for i, t in parts]
    stores = [pltpu.make_async_copy(held.at[i, t], refs[count + i].at[0, 0, t], sems.at[1, i, t]) for i, t in parts]
    for load in loads:
        load.start()
    for load, store in zip(loads, stores):
        load.wait()
        store.start()
    for store in stores:
        store.wait()


def on_device(frames, queries, keys, values, grad_out, windows):
    heads = queries.shape[-1] // HD
    most = (heads // 2 + 1) // 2
    near = (most, TILES, TILE, HD)
    wide = (most, 3, TILES, TILE, HD)
    both = (most, 2, TILES, TILE, HD)
    bf16 = functools.partial(pltpu.VMEM, dtype=jnp.bfloat16)
    f32 = functools.partial(pltpu.VMEM, dtype=jnp.float32)
    rows = TILES * TILE
    dma = pltpu.SemaphoreType.DMA
    anywhere = pl.BlockSpec(memory_space=pl.ANY)
    results = pl.pallas_call(
        functools.partial(kernel, frames, heads),
        name="window_attention",
        out_shape=[jax.ShapeDtypeStruct(queries.shape, jnp.bfloat16)] * 4,
        in_specs=[pl.BlockSpec(memory_space=pltpu.SMEM)] + [anywhere] * 4,
        out_specs=[anywhere] * 4,
        scratch_shapes=[
            bf16(near), bf16(near), bf16(wide), bf16(wide), f32((BANDS, 3 * TILES, ROWS)),
            f32((most, rows, HD)), f32((most, rows, HD)), f32((2, rows, HD)), f32((2, rows, HD)),
            bf16(both), bf16(both), bf16(both), bf16(both),
            bf16(near), bf16(near), bf16(near), bf16(near),
            dma((4, most, 4)), dma((4, most, 4)), dma((4, most)),
            dma((2, most, 2, 4)), dma((2, most, 2, 4)), dma((2, most, 2, 2)), dma((2, most, 2, 2)),
            dma((4, most, 4)), dma((4, most, 4)), dma((4, most)), dma((4,)), dma((4,)),
            f32((3 * TILES, ROWS)),
        ],
        cost_estimate=pl.CostEstimate(flops=8 * 10**9, bytes_accessed=8 * 10**6, transcendentals=4 * 10**6),
        compiler_params=pltpu.CompilerParams(
            collective_id=0, has_side_effects=True, vmem_limit_bytes=56 * 2**20
        ),
    )(windows, queries, keys, values, grad_out)
    return pl.pallas_call(
        copy_kernel,
        name="copy_out",
        out_shape=[jax.ShapeDtypeStruct(queries.shape, jnp.bfloat16)] * 4,
        in_specs=[anywhere] * 4,
        out_specs=[anywhere] * 4,
        scratch_shapes=[bf16((4, *queries.shape[2:])), dma((2, 4, WT))],
    )(*results)


def solution(mesh):
    placed = P("frame", "band", None, None, None)
    return jax.shard_map(
        functools.partial(on_device, mesh.shape["frame"]),
        mesh=mesh,
        in_specs=(placed, placed, placed, placed, P("frame", "band", None, None)),
        out_specs=(placed, placed, placed, placed),
        check_vma=False,
    )
```
